1024 devices in a mesh: kgrp: 16 (over x, z_hi), row: 8 (over z_lo, core), col: 8 (over y).
Axes of the slice: x: 8, y: 8, z: 8 (z_hi: 2, z_lo: 4; z = z_hi * 4 + z_lo), core: 2. Of those that a mesh axis runs over, the one named last changes fastest.
Arguments:
- occ_orbitals: bfloat16 [32, 1024, 2, 512], P('kgrp', ('row', 'col')), may hold values from -5 to 5
- emp_orbitals: bfloat16 [32, 1024, 2, 512], P('kgrp', ('row', 'col')), may hold values from -5 to 5
- energies: float32 [2, 32, 512], replicated, may hold values from 0.05 to 1.5
- band_order: int32 [2, 32, 512], replicated, may hold values from 0 to 511, each once within a row
- imag_times: float32 [2], replicated, may hold values from 0.3 to 3
- kq_map: int32 [2, 32], replicated, may hold values from 0 to 31, each once within a row
- slot_kpoint: int32 [32], replicated, may hold values from 0 to 31, each once
Outputs:
- suscept: float32 [2, 2, 8, 128, 2, 1024], P(None, None, 'col', 'kgrp', None, 'row')
The draws below stay inside these ranges and needn't reach their ends.
Inputs may be any that keep to these rules, and one draw needn't show every extreme that they name: `kq_map`: each row is a permutation of the k-point ids. `slot_kpoint`: a permutation of the k-point ids. `band_order`: each row over the last dimension is a permutation of the ranks.
All inputs are finite; a program needn't handle non-finite values.
Results may differ from the reference program's by a relative error of at most 0.0003.
Values may be sent and summed in bfloat16 or wider, within the bound.
A program may use at most 32 MiB of HBM per device.

```python
import math
import jax
import jax.numpy as jnp
from jax import lax

NB = 512
NMU = 1024
NQ = 2
NT = 2
K = 32
N_ROW = 8
N_COL = 8


def block_levels(key, shape, pieces, smallest, largest):
    def one(dim, shards_of):
        heights = jax.random.uniform(jax.random.fold_in(jax.random.fold_in(key, 6), dim), (shards_of,), jnp.float32, smallest / len(pieces), largest / len(pieces))
        return jnp.repeat(jnp.exp(heights), shape[dim] // shards_of).reshape((-1,) + (1,) * (len(shape) - dim - 1))

    factor_of = one(*pieces[0])
    for cut in pieces[1:]:
        factor_of = factor_of * one(*cut)
    return factor_of


def centred(stream_key, shape, spread, bound, split=(), held_as=jnp.bfloat16):
    drawn = spread * jax.random.normal(stream_key, shape, jnp.float32)
    if split:
        drawn = drawn * block_levels(stream_key, shape, split, -0.22, 0.18)
    return jnp.clip(drawn, -bound, bound).astype(held_as)


def setup_inputs(seed: int = 0) -> dict:
    arg_keys = jax.random.split(jax.random.key(seed), 8)
    return {
        "occ_orbitals": centred(arg_keys[0], (K, NMU, 2, NB), 0.35, 5.0, ((0, 16), (1, 64))),
        "emp_orbitals": centred(arg_keys[1], (K, NMU, 2, NB), 0.35, 5.0, ((0, 16), (1, 64))),
        "energies": jnp.clip(jnp.exp(jax.random.uniform(arg_keys[2], (2, K, NB), jnp.float32, math.log(0.05), math.log(1.5))), 0.05, 1.5),
        "band_order": jax.vmap(lambda own: jax.random.permutation(own, NB))(jax.random.split(arg_keys[3], 2 * K)).reshape((2, K, NB)).astype(jnp.int32),
        "imag_times": jnp.clip(jnp.exp(jax.random.uniform(arg_keys[4], (NT,), jnp.float32, math.log(0.3), math.log(3.0))), 0.3, 3.0),
        "kq_map": jax.vmap(lambda own: jax.random.permutation(own, K))(jax.random.split(arg_keys[5], NQ)).reshape((NQ, K)).astype(jnp.int32),
        "slot_kpoint": jax.random.permutation(arg_keys[6], K).astype(jnp.int32),
    }


def band_weights(levels, band_rank, imag_times):
    picked = jnp.take_along_axis(levels, band_rank.astype(jnp.int32), axis=0)
    return jnp.exp(-picked[None, :] * imag_times[:, None])


def green_tile(row_panel, col_panel, weights):
    times_count = weights.shape[0]
    scaled = (row_panel[None] * weights[:, None, None, :]).astype(jnp.bfloat16)
    scaled = scaled.reshape(times_count, row_panel.shape[0], -1)
    turned = jnp.concatenate([-col_panel[:, 1], col_panel[:, 0]], axis=1)
    stacked = jnp.concatenate([col_panel.reshape(col_panel.shape[0], -1), turned], axis=0)
    result = lax.dot_general(stacked, scaled, (((1,), (2,)), ((), ())), preferred_element_type=jnp.float32)
    return result.reshape(2, col_panel.shape[0], times_count, row_panel.shape[0])


def pair_term(held_tile, moved_tile, factor):
    real_part = held_tile[0] * moved_tile[0] + held_tile[1] * moved_tile[1]
    imag_part = held_tile[1] * moved_tile[0] - held_tile[0] * moved_tile[1]
    return factor * jnp.stack([real_part, imag_part])


def reference(occ_orbitals, emp_orbitals, energies, band_order, imag_times, kq_map, slot_kpoint):
    kpoints = occ_orbitals.shape[0]
    positions = jnp.arange(kpoints, dtype=jnp.int32)
    inverse = jnp.zeros((kpoints,), jnp.int32).at[slot_kpoint].set(positions)
    sources = inverse[kq_map[:, slot_kpoint]]
    factor = -1.0 / kpoints

    def advance(suscept, slot_index):
        held_tile = green_tile(occ_orbitals[slot_index], occ_orbitals[slot_index],
                               band_weights(energies[0, slot_index], band_order[0, slot_index], imag_times))
        pair_terms = []
        for transfer in range(NQ):
            source = sources[transfer, slot_index]
            moved_tile = green_tile(emp_orbitals[source], emp_orbitals[source],
                                    band_weights(energies[1, source], band_order[1, source], imag_times))
            pair_terms.append(pair_term(held_tile, moved_tile, factor))
        return suscept + jnp.stack(pair_terms, axis=1), None

    initial = jnp.zeros((2, NQ, NMU, NT, NMU), jnp.float32)
    suscept, unused = lax.scan(advance, initial, positions)
    suscept = suscept.reshape(2, NQ, N_ROW, N_COL, NMU // (N_ROW * N_COL), NT, NMU)
    suscept = jnp.transpose(suscept, (0, 1, 3, 2, 4, 5, 6))
    return suscept.reshape(2, NQ, N_COL, NMU // N_COL, NT, NMU)
```

```python
import functools

import jax
import jax.numpy as jnp
from jax import lax
from jax.experimental import pallas as pl
from jax.experimental.pallas import tpu as pltpu
from jax.sharding import PartitionSpec as P

MESH = pl.DeviceIdType.MESH
CORES = 2
NEAR = (2, -2, 1, -1)


def band_weights(energies, band_order, imag_times, slots):
    levels = jnp.concatenate([energies[s, pl.ds(j, 1)] for s, j in slots], axis=0)
    ranks = jnp.concatenate([band_order[s, pl.ds(j, 1)] for s, j in slots], axis=0)
    levels = jnp.concatenate([levels, levels], axis=0)
    ranks = jnp.concatenate([ranks, ranks], axis=0)
    bands = levels.shape[1]
    picked = []
    for b in range(bands // 128):
        rank = ranks[:, b * 128 : (b + 1) * 128]
        lane = rank % 128
        found = jnp.zeros(rank.shape, jnp.float32)
        for c in range(bands // 128):
            taken = jnp.take_along_axis(levels[:, c * 128 : (c + 1) * 128], lane, axis=1)
            found = jnp.where(rank // 128 == c, taken, found)
        picked.append(found)
    picked = jnp.concatenate(picked, axis=1)
    return [jnp.exp(-picked * imag_times[t]) for t in range(2)]


def kernel(
    sizes,
    own_ref,
    energies,
    band_order,
    imag_times,
    kq_map,
    slot_kpoint,
    out_ref,
    rows,
    cols,
    packed,
    landed,
    inverse,
    row_send,
    row_recv,
    col_send,
    col_recv,
    mate_send,
    mate_recv,
    tile_send,
    tile_recv,
    local_sem,
):
    groups, row_count, col_count = sizes
    xs, line = groups // 2, row_count // CORES
    per_group = own_ref.shape[1]
    kpoints = groups * per_group
    group, row, y = lax.axis_index("kgrp"), lax.axis_index("row"), lax.axis_index("col")
    x, zh = group // 2, group % 2
    zl, core = row // CORES, row % CORES

    def along_y(step):
        return (group, row, lax.rem(y + step + col_count, col_count))

    def along_z(step):
        return (group, lax.rem(zl + step, line) * CORES + core, y)

    mate = (group, zl * CORES + 1 - core, y)
    others = [(dx, dz) for dx in (4, 3, 5, 2, 6, 1, 7, 0) for dz in (1, 0) if dx or dz]

    def group_at(dx, dz):
        return lax.rem(x + dx, xs) * 2 + lax.rem(zh + dz, 2)

    peers = [along_y(s) for s in NEAR] + [along_z(e) for e in range(1, line)] + [mate]
    peers += [(group_at(dx, dz), row, y) for dx, dz in others]
    barrier = pltpu.get_barrier_semaphore()
    for peer in peers:
        pl.semaphore_signal(barrier, inc=1, device_id=peer, device_id_type=MESH)

    mine = []
    for kind in range(2):
        for i, target in enumerate((rows.at[kind, y], cols.at[kind, row])):
            mine.append(
                pltpu.make_async_copy(own_ref.at[kind], target, local_sem.at[kind * 2 + i])
            )
    for copy in mine:
        copy.start()
    slots = [(s, group * per_group + p) for s in range(2) for p in range(per_group)]
    weights = band_weights(energies, band_order, imag_times, slots)

    def find(k, carry):
        total = jnp.int32(0)
        for s in range(kpoints):
            total = jnp.where(slot_kpoint[s] == k, s, total)
        inverse[k] = total
        return carry

    pl.semaphore_wait(barrier, len(peers))

    row_copies, col_copies, mate_copies, tile_copies = {}, {}, {}, {}

    def send_rows(kind, distance, step):
        source = lax.rem(y - (distance - step) + col_count, col_count)
        key = (kind, distance % col_count)
        held = own_ref.at[kind] if distance == step else rows.at[kind, source]
        row_copies[key] = pltpu.make_async_remote_copy(
            src_ref=held,
            dst_ref=rows.at[kind, source],
            send_sem=row_send.at[key[0], key[1]],
            recv_sem=row_recv.at[key[0], key[1]],
            device_id=along_y(step),
            device_id_type=MESH,
        )
        row_copies[key].start()

    def send_cols(kind, step):
        col_copies[kind, step] = pltpu.make_async_remote_copy(
            src_ref=own_ref.at[kind],
            dst_ref=cols.at[kind, row],
            send_sem=col_send.at[kind, step],
            recv_sem=col_recv.at[kind, step],
            device_id=along_z(step),
            device_id_type=MESH,
        )
        col_copies[kind, step].start()

    def send_mate(kind, step):
        source = lax.rem(zl - step + line, line) * CORES + core
        mate_copies[kind, step] = pltpu.make_async_remote_copy(
            src_ref=cols.at[kind, source] if step else own_ref.at[kind],
            dst_ref=cols.at[kind, source],
            send_sem=mate_send.at[kind, step],
            recv_sem=mate_recv.at[kind, step],
            device_id=mate,
            device_id_type=MESH,
        )
        mate_copies[kind, step].start()

    for kind in range(2):
        for step in NEAR[:2]:
            send_rows(kind, step, step)
        for step in (2, 3, 1):
            send_cols(kind, step)
        for step in NEAR[2:]:
            send_rows(kind, step, step)
        send_mate(kind, 0)
    lax.fori_loop(0, kpoints, find, 0)
    for kind in range(2):
        for sign in (1, -1):
            row_copies[kind, 2 * sign % col_count].wait_recv()
            if (sign == 1) == (kind == 0):
                send_rows(kind, 4 * sign, 2 * sign)
            send_rows(kind, 3 * sign, sign)
        for step in (1, 2, 3):
            col_copies[kind, step].wait_recv()
            send_mate(kind, step)

    for copy in mine:
        copy.wait()
    for kind in range(2):
        for distance in (1, 7, 3, 5, 4):
            row_copies[kind, distance].wait_recv()
        for step in range(line):
            mate_copies[kind, step].wait_recv()
        for slot in range(per_group):
            panel = rows[kind, :, slot].reshape(-1, own_ref.shape[-1])
            others_panel = cols[kind, :, slot].reshape(-1, own_ref.shape[-1])
            bands = panel.shape[1] // 2
            w = [weights[t][kind * per_group + slot : kind * per_group + slot + 1] for t in range(2)]
            wide = panel.astype(jnp.float32)
            scaled = jnp.concatenate(
                [wide * jnp.concatenate([w[t], w[t]], axis=1) for t in range(2)], axis=0
            ).astype(jnp.bfloat16)
            turned = jnp.concatenate([-others_panel[:, bands:], others_panel[:, :bands]], axis=1)
            stacked = jnp.concatenate([others_panel, turned], axis=0)
            tile = lax.dot_general(
                stacked, scaled, (((1,), (1,)), ((), ())), preferred_element_type=jnp.float32
            )
            count = panel.shape[0]
            for comp in range(2):
                for t in range(2):
                    part = tile[comp * count : (comp + 1) * count, t * count : (t + 1) * count]
                    packed[kind, :, slot, comp, t] = part.reshape(groups, -1, count)
        for n, (dx, dz) in enumerate(others):
            there = group_at(dx, dz)
            tile_copies[kind, n] = pltpu.make_async_remote_copy(
                src_ref=packed.at[kind, there],
                dst_ref=landed.at[kind, pl.ds(group * per_group, per_group)],
                send_sem=tile_send.at[kind, n],
                recv_sem=tile_recv.at[kind, n],
                device_id=(there, row, y),
                device_id_type=MESH,
            )
            tile_copies[kind, n].start()
        landed[kind, pl.ds(group * per_group, per_group)] = packed[kind, group]

    for copy in (*row_copies.values(), *col_copies.values(), *mate_copies.values()):
        copy.wait_send()
    for copy in tile_copies.values():
        copy.wait_recv()

    def add(j, totals):
        held_re, held_im = landed[0, j, 0], landed[0, j, 1]
        kpoint = slot_kpoint[j]
        new = []
        for q in range(2):
            source = inverse[kq_map[q, kpoint]]
            moved_re, moved_im = landed[1, source, 0], landed[1, source, 1]
            new.append(totals[2 * q] + (held_re * moved_re + held_im * moved_im))
            new.append(totals[2 * q + 1] + (held_im * moved_re - held_re * moved_im))
        return tuple(new)

    zero = jnp.zeros(landed.shape[3:], jnp.float32)
    totals = lax.fori_loop(0, kpoints, add, (zero,) * 4)
    for q in range(2):
        for comp in range(2):
            out_ref[comp, q] = totals[2 * q + comp] * (-1.0 / kpoints)
    for copy in tile_copies.values():
        copy.wait_send()


def shards(sizes, occ, emp, energies, band_order, imag_times, kq_map, slot_kpoint):
    groups, row_count, col_count = sizes
    per_group, chunk = occ.shape[:2]
    width = occ.shape[2] * occ.shape[3]
    points = row_count * chunk
    share = points // groups
    own = jnp.stack([occ, emp]).reshape(2, per_group, chunk, width)
    vmem, smem = pl.BlockSpec(memory_space=pltpu.VMEM), pl.BlockSpec(memory_space=pltpu.SMEM)
    dma = pltpu.SemaphoreType.DMA
    result = pl.pallas_call(
        functools.partial(kernel, sizes),
        out_shape=jax.ShapeDtypeStruct((2, 2, 2, share, points), jnp.float32),
        in_specs=[vmem, vmem, vmem, smem, smem, smem],
        out_specs=vmem,
        scratch_shapes=[
            pltpu.VMEM((2, col_count, per_group, chunk, width), jnp.bfloat16),
            pltpu.VMEM((2, row_count, per_group, chunk, width), jnp.bfloat16),
            pltpu.VMEM((2, groups, per_group, 2, 2, share, points), jnp.float32),
            pltpu.VMEM((2, groups * per_group, 2, 2, share, points), jnp.float32),
            pltpu.SMEM((groups * per_group,), jnp.int32),
            dma((2, col_count)),
            dma((2, col_count)),
            dma((2, 4)),
            dma((2, 4)),
            dma((2, 4)),
            dma((2, 4)),
            dma((2, 16)),
            dma((2, 16)),
            dma((4,)),
        ],
        compiler_params=pltpu.CompilerParams(collective_id=0, has_side_effects=True),
        name="polarizability",
    )(own, energies, band_order, imag_times, kq_map, slot_kpoint)
    return jnp.transpose(result, (0, 1, 3, 2, 4))[:, :, None]


def solution(mesh):
    sizes = (mesh.shape["kgrp"], mesh.shape["row"], mesh.shape["col"])
    in_specs = (
        P("kgrp", ("row", "col"), None, None),
        P("kgrp", ("row", "col"), None, None),
        P(),
        P(),
        P(),
        P(),
        P(),
    )
    out_specs = P(None, None, "col", "kgrp", None, "row")
    return jax.shard_map(
        functools.partial(shards, sizes),
        mesh=mesh,
        in_specs=in_specs,
        out_specs=out_specs,
        check_vma=False,
    )
```

```python
import functools

import jax
import jax.numpy as jnp
from jax import lax
from jax.experimental import pallas as pl
from jax.experimental.pallas import tpu as pltpu
from jax.sharding import PartitionSpec as P

MESH = pl.DeviceIdType.MESH
CORES = 2
LANES = 128
NEAR = (2, -2, 1, -1)
TOP = 32767.0


def band_weights(levels, ranks, imag_times):
    pieces = levels.shape[1] // LANES
    picked = []
    for b in range(pieces):
        rank = ranks[:, b * LANES : (b + 1) * LANES]
        lane = rank % LANES
        found = jnp.zeros(rank.shape, jnp.float32)
        for c in range(pieces):
            taken = jnp.take_along_axis(levels[:, c * LANES : (c + 1) * LANES], lane, axis=1)
            found = jnp.where(rank // LANES == c, taken, found)
        picked.append(found)
    picked = jnp.concatenate(picked, axis=1)
    return [jnp.exp(-picked * imag_times[t]) for t in range(2)]


def kernel(
    sizes,
    occ_hbm,
    emp_hbm,
    energies_hbm,
    order_hbm,
    times_hbm,
    kq_hbm,
    kpoint_hbm,
    out_ref,
    raw,
    levels,
    ranks,
    rows,
    cols,
    packed,
    landed,
    decoded,
    imag_times,
    kq_map,
    slot_kpoint,
    inverse,
    row_send,
    row_recv,
    col_send,
    col_recv,
    mate_send,
    mate_recv,
    tile_send,
    tile_recv,
    local_sem,
):
    groups, row_count, col_count = sizes
    xs, line = groups // 2, row_count // CORES
    per_group = raw.shape[1]
    bands = raw.shape[4]
    kpoints = groups * per_group
    group, row, y = lax.axis_index("kgrp"), lax.axis_index("row"), lax.axis_index("col")
    x, zh = group // 2, group % 2
    zl, core = row // CORES, row % CORES

    def along_y(step):
        return (group, row, lax.rem(y + step + col_count, col_count))

    def along_z(step):
        return (group, lax.rem(zl + step, line) * CORES + core, y)

    mate = (group, zl * CORES + 1 - core, y)
    others = [(dx, dz) for dx in (4, 3, 5, 2, 6, 1, 7, 0) for dz in (1, 0) if dx or dz]

    def group_at(dx, dz):
        return lax.rem(x + dx, xs) * 2 + lax.rem(zh + dz, 2)

    peers = [(group_at(dx, dz), row, y) for dx, dz in others]
    peers += [along_z(e) for e in range(1, line)] + [along_y(s) for s in NEAR] + [mate]
    barrier = pltpu.get_barrier_semaphore()
    for peer in peers:
        pl.semaphore_signal(barrier, inc=1, device_id=peer, device_id_type=MESH)

    own = pl.ds(group * per_group, per_group)
    fetches = [
        pltpu.make_async_copy(occ_hbm, raw.at[0], local_sem.at[0]),
        pltpu.make_async_copy(emp_hbm, raw.at[1], local_sem.at[1]),
        pltpu.make_async_copy(times_hbm, imag_times, local_sem.at[2]),
        pltpu.make_async_copy(kq_hbm, kq_map, local_sem.at[3]),
        pltpu.make_async_copy(kpoint_hbm, slot_kpoint, local_sem.at[4]),
    ]
    for kind in range(2):
        part = pl.ds(kind * per_group, per_group)
        fetches += [
            pltpu.make_async_copy(
                energies_hbm.at[kind, own], levels.at[part], local_sem.at[5 + kind]
            ),
            pltpu.make_async_copy(order_hbm.at[kind, own], ranks.at[part], local_sem.at[7 + kind]),
        ]
    for copy in fetches:
        copy.start()
    for copy in fetches:
        copy.wait()
    for kind in range(2):
        for slot in range(per_group):
            for part in range(2):
                piece = raw[kind, slot, :, part, :]
                span = slice(part * bands, (part + 1) * bands)
                rows[kind, y, slot, :, span] = piece
                cols[kind, row, slot, :, span] = piece

    pl.semaphore_wait(barrier, len(peers))

    row_copies, col_copies, mate_copies, tile_copies = {}, {}, {}, {}

    def send_rows(kind, distance, step):
        source = lax.rem(y - (distance - step) + col_count, col_count)
        key = (kind, distance % col_count)
        row_copies[key] = pltpu.make_async_remote_copy(
            src_ref=rows.at[kind, source],
            dst_ref=rows.at[kind, source],
            send_sem=row_send.at[key[0], key[1]],
            recv_sem=row_recv.at[key[0], key[1]],
            device_id=along_y(step),
            device_id_type=MESH,
        )
        row_copies[key].start()

    def send_cols(kind, step):
        col_copies[kind, step] = pltpu.make_async_remote_copy(
            src_ref=cols.at[kind, row],
            dst_ref=cols.at[kind, row],
            send_sem=col_send.at[kind, step],
            recv_sem=col_recv.at[kind, step],
            device_id=along_z(step),
            device_id_type=MESH,
        )
        col_copies[kind, step].start()

    def send_mate(kind, step):
        source = lax.rem(zl - step + line, line) * CORES + core
        mate_copies[kind, step] = pltpu.make_async_remote_copy(
            src_ref=cols.at[kind, source],
            dst_ref=cols.at[kind, source],
            send_sem=mate_send.at[kind, step],
            recv_sem=mate_recv.at[kind, step],
            device_id=mate,
            device_id_type=MESH,
        )
        mate_copies[kind, step].start()

    for kind in range(2):
        for step in NEAR[:2]:
            send_rows(kind, step, step)
        for step in (2, 3, 1):
            send_cols(kind, step)
        for step in NEAR[2:]:
            send_rows(kind, step, step)
        send_mate(kind, 0)

    def find(k, carry):
        slot = jnp.int32(0)
        for s in range(kpoints):
            slot = jnp.where(slot_kpoint[s] == k, s, slot)
        inverse[k] = slot
        return carry

    lax.fori_loop(0, kpoints, find, 0)
    twice = [jnp.concatenate([ref[...], ref[...]], axis=0) for ref in (levels, ranks)]
    weights = band_weights(*twice, imag_times)

    for kind in range(2):
        for sign in (1, -1):
            row_copies[kind, 2 * sign % col_count].wait_recv()
            if (sign == 1) == (kind == 0):
                send_rows(kind, 4 * sign, 2 * sign)
            send_rows(kind, 3 * sign, sign)
        for step in (1, 2, 3):
            col_copies[kind, step].wait_recv()
            send_mate(kind, step)

    points = row_count * raw.shape[2]
    share = points // groups
    lanes = lax.broadcasted_iota(jnp.int32, (points, LANES), 1)
    for kind in range(2):
        for distance in (1, 7, 3, 5, 4):
            row_copies[kind, distance].wait_recv()
        for step in range(line):
            mate_copies[kind, step].wait_recv()
        powers = jnp.zeros((points, LANES), jnp.float32)
        for slot in range(per_group):
            row_panel = rows[kind, :, slot].reshape(-1, 2 * bands)
            col_panel = cols[kind, :, slot].reshape(-1, 2 * bands)
            at = kind * per_group + slot
            w = [weights[t][at : at + 1] for t in range(2)]
            wide = row_panel.astype(jnp.float32)
            scaled = jnp.concatenate(
                [wide * jnp.concatenate([w[t], w[t]], axis=1) for t in range(2)], axis=0
            ).astype(jnp.bfloat16)
            turned = jnp.concatenate([-col_panel[:, bands:], col_panel[:, :bands]], axis=1)
            stacked = jnp.concatenate([col_panel, turned], axis=0)
            tile = lax.dot_general(
                stacked, scaled, (((1,), (1,)), ((), ())), preferred_element_type=jnp.float32
            )
            for t in range(2):
                span = slice(t * LANES, (t + 1) * LANES)
                pair = [tile[:points, span], tile[points:, span]]
                largest = jnp.maximum(jnp.abs(pair[0]), jnp.abs(pair[1]))
                largest = jnp.maximum(jnp.max(largest, axis=1, keepdims=True), 1e-30)
                power = jnp.floor(jnp.log2(largest)) + 1.0
                unit = jnp.exp2(15.0 - power)
                powers = jnp.where(lanes == slot * 2 + t, power, powers)
                for comp in range(2):
                    value = jnp.clip(jnp.round(pair[comp] * unit), -TOP, TOP).astype(jnp.int16)
                    packed[kind, :, slot * 2 + t, comp * share : (comp + 1) * share] = (
                        value.reshape(groups, share, LANES)
                    )
        coded = powers.astype(jnp.int16).reshape(groups, share, LANES)
        for comp in range(2):
            packed[kind, :, 2 * per_group, comp * share : (comp + 1) * share] = coded
        for n, (dx, dz) in enumerate(others):
            there = group_at(dx, dz)
            tile_copies[kind, n] = pltpu.make_async_remote_copy(
                src_ref=packed.at[kind, there],
                dst_ref=landed.at[kind, group],
                send_sem=tile_send.at[kind, n],
                recv_sem=tile_recv.at[kind, n],
                device_id=(there, row, y),
                device_id_type=MESH,
            )
            tile_copies[kind, n].start()

    for copy in (*row_copies.values(), *col_copies.values(), *mate_copies.values()):
        copy.wait_send()

    def decode(kind, held, source):
        unit = jnp.exp2(held[kind, source, 2 * per_group].astype(jnp.float32) - 15.0)
        for slot in range(per_group):
            for t in range(2):
                k = slot * 2 + t
                value = held[kind, source, k].astype(jnp.float32) * unit[:, k : k + 1]
                decoded[kind, source * per_group + slot, t] = value

    for kind in range(2):
        decode(kind, packed, group)
        for n, (dx, dz) in reversed(list(enumerate(others))):
            tile_copies[kind, n].wait_recv()
            decode(kind, landed, group_at(-dx % xs, dz))

    def add(j, totals):
        held = decoded[0, j]
        held_re, held_im = held[:, :share], held[:, share:]
        kpoint = slot_kpoint[j]
        new = []
        for q in range(2):
            moved = decoded[1, inverse[kq_map[q, kpoint]]]
            moved_re, moved_im = moved[:, :share], moved[:, share:]
            new.append(totals[2 * q] + (held_re * moved_re + held_im * moved_im))
            new.append(totals[2 * q + 1] + (held_im * moved_re - held_re * moved_im))
        return tuple(new)

    zero = jnp.zeros((2, share, LANES), jnp.float32)
    totals = lax.fori_loop(0, kpoints, add, (zero,) * 4)
    for q in range(2):
        for comp in range(2):
            for t in range(2):
                out_ref[comp, q, 0, :, t, :] = totals[2 * q + comp][t] * (-1.0 / kpoints)
    for copy in tile_copies.values():
        copy.wait_send()


def shards(sizes, occ, emp, energies, band_order, imag_times, kq_map, slot_kpoint):
    groups, row_count, col_count = sizes
    per_group, chunk, parts, bands = occ.shape
    width = parts * bands
    share = row_count * chunk // groups
    kpoints = groups * per_group
    dma = pltpu.SemaphoreType.DMA
    return pl.pallas_call(
        functools.partial(kernel, sizes),
        out_shape=jax.ShapeDtypeStruct((2, 2, 1, share, 2, col_count * chunk), jnp.float32),
        in_specs=[pl.BlockSpec(memory_space=pl.ANY)] * 7,
        out_specs=pl.BlockSpec(memory_space=pltpu.VMEM),
        scratch_shapes=[
            pltpu.VMEM((2, *occ.shape), jnp.bfloat16),
            pltpu.VMEM((2 * per_group, bands), jnp.float32),
            pltpu.VMEM((2 * per_group, bands), jnp.int32),
            pltpu.VMEM((2, col_count, per_group, chunk, width), jnp.bfloat16),
            pltpu.VMEM((2, row_count, per_group, chunk, width), jnp.bfloat16),
            pltpu.VMEM((2, groups, 2 * per_group + 1, 2 * share, LANES), jnp.int16),
            pltpu.VMEM((2, groups, 2 * per_group + 1, 2 * share, LANES), jnp.int16),
            pltpu.VMEM((2, kpoints, 2, 2 * share, LANES), jnp.float32),
            pltpu.SMEM(imag_times.shape, jnp.float32),
            pltpu.SMEM(kq_map.shape, jnp.int32),
            pltpu.SMEM(slot_kpoint.shape, jnp.int32),
            pltpu.SMEM((kpoints,), jnp.int32),
            dma((2, col_count)),
            dma((2, col_count)),
            dma((2, 4)),
            dma((2, 4)),
            dma((2, 4)),
            dma((2, 4)),
            dma((2, groups)),
            dma((2, groups)),
            dma((9,)),
        ],
        compiler_params=pltpu.CompilerParams(collective_id=0, has_side_effects=True),
        name="polarizability",
    )(occ, emp, energies, band_order, imag_times, kq_map, slot_kpoint)


def solution(mesh):
    sizes = (mesh.shape["kgrp"], mesh.shape["row"], mesh.shape["col"])
    in_specs = (
        P("kgrp", ("row", "col"), None, None),
        P("kgrp", ("row", "col"), None, None),
        P(),
        P(),
        P(),
        P(),
        P(),
    )
    out_specs = P(None, None, "col", "kgrp", None, "row")
    return jax.shard_map(
        functools.partial(shards, sizes),
        mesh=mesh,
        in_specs=in_specs,
        out_specs=out_specs,
        check_vma=False,
    )
```

```python
import functools

import jax
import jax.numpy as jnp
from jax import lax
from jax.experimental import pallas as pl
from jax.experimental.pallas import tpu as pltpu
from jax.sharding import PartitionSpec as P

MESH = pl.DeviceIdType.MESH
CORES = 2
LANES = 128
NEAR = (2, -2, 1, -1)
TOP = 32767.0
RELAY = ((1, -1), (2, -2), (1, -1))


def band_weights(levels, ranks, imag_times):
    pieces = levels.shape[1] // LANES
    picked = []
    for b in range(pieces):
        rank = ranks[:, b * LANES : (b + 1) * LANES]
        lane = rank % LANES
        found = jnp.zeros(rank.shape, jnp.float32)
        for c in range(pieces):
            taken = jnp.take_along_axis(levels[:, c * LANES : (c + 1) * LANES], lane, axis=1)
            found = jnp.where(rank // LANES == c, taken, found)
        picked.append(found)
    picked = jnp.concatenate(picked, axis=1)
    return [jnp.exp(-picked * imag_times[t]) for t in range(2)]


def kernel(
    sizes,
    occ_hbm,
    emp_hbm,
    energies_hbm,
    order_hbm,
    times_hbm,
    kq_hbm,
    kpoint_hbm,
    out_ref,
    raw,
    levels,
    ranks,
    rows,
    cols,
    packed,
    landed,
    decoded,
    imag_times,
    kq_map,
    slot_kpoint,
    inverse,
    row_send,
    row_recv,
    col_send,
    col_recv,
    mate_send,
    mate_recv,
    tile_send,
    tile_recv,
    local_sem,
    relay_sem,
):
    groups, row_count, col_count = sizes
    xs, line = groups // 2, row_count // CORES
    per_group = raw.shape[1]
    bands = raw.shape[4]
    kpoints = groups * per_group
    group, row, y = lax.axis_index("kgrp"), lax.axis_index("row"), lax.axis_index("col")
    x, zh = group // 2, group % 2
    zl, core = row // CORES, row % CORES

    def along_y(step):
        return (group, row, lax.rem(y + step + col_count, col_count))

    def along_z(step):
        return (group, lax.rem(zl + step, line) * CORES + core, y)

    mate = (group, zl * CORES + 1 - core, y)
    others = [(dx, dz) for dx in (4, 3, 5, 2, 6, 1, 7, 0) for dz in (1, 0) if dx or dz]

    def group_at(dx, dz):
        return lax.rem(x + dx, xs) * 2 + lax.rem(zh + dz, 2)

    def along_x(dx, dz=0):
        return (group_at(dx % xs, dz), row, y)

    peers = [along_x(0, 1), along_x(1), along_x(-1)]
    peers += [along_z(e) for e in range(1, line)] + [along_y(s) for s in NEAR] + [mate]
    barrier = pltpu.get_barrier_semaphore()
    for peer in peers:
        pl.semaphore_signal(barrier, inc=1, device_id=peer, device_id_type=MESH)

    own = pl.ds(group * per_group, per_group)
    fetches = [
        pltpu.make_async_copy(occ_hbm, raw.at[0], local_sem.at[0]),
        pltpu.make_async_copy(emp_hbm, raw.at[1], local_sem.at[1]),
        pltpu.make_async_copy(times_hbm, imag_times, local_sem.at[2]),
        pltpu.make_async_copy(kq_hbm, kq_map, local_sem.at[3]),
        pltpu.make_async_copy(kpoint_hbm, slot_kpoint, local_sem.at[4]),
    ]
    for kind in range(2):
        part = pl.ds(kind * per_group, per_group)
        fetches += [
            pltpu.make_async_copy(
                energies_hbm.at[kind, own], levels.at[part], local_sem.at[5 + kind]
            ),
            pltpu.make_async_copy(order_hbm.at[kind, own], ranks.at[part], local_sem.at[7 + kind]),
        ]
    for copy in fetches:
        copy.start()
    for copy in fetches:
        copy.wait()
    for kind in range(2):
        for slot in range(per_group):
            for part in range(2):
                piece = raw[kind, slot, :, part, :]
                span = slice(part * bands, (part + 1) * bands)
                rows[kind, y, slot, :, span] = piece
                cols[kind, row, slot, :, span] = piece

    pl.semaphore_wait(barrier, len(peers))

    def relay(stage):
        if stage:
            pl.semaphore_wait(relay_sem.at[stage - 1], len(RELAY[stage - 1]))
        if stage < len(RELAY):
            for dx in RELAY[stage]:
                pl.semaphore_signal(
                    relay_sem.at[stage], inc=1, device_id=along_x(dx), device_id_type=MESH
                )

    relay(0)

    row_copies, col_copies, mate_copies, tile_copies = {}, {}, {}, {}

    def send_rows(kind, distance, step):
        source = lax.rem(y - (distance - step) + col_count, col_count)
        key = (kind, distance % col_count)
        row_copies[key] = pltpu.make_async_remote_copy(
            src_ref=rows.at[kind, source],
            dst_ref=rows.at[kind, source],
            send_sem=row_send.at[key[0], key[1]],
            recv_sem=row_recv.at[key[0], key[1]],
            device_id=along_y(step),
            device_id_type=MESH,
        )
        row_copies[key].start()

    def send_cols(kind, step):
        col_copies[kind, step] = pltpu.make_async_remote_copy(
            src_ref=cols.at[kind, row],
            dst_ref=cols.at[kind, row],
            send_sem=col_send.at[kind, step],
            recv_sem=col_recv.at[kind, step],
            device_id=along_z(step),
            device_id_type=MESH,
        )
        col_copies[kind, step].start()

    def send_mate(kind, step):
        source = lax.rem(zl - step + line, line) * CORES + core
        mate_copies[kind, step] = pltpu.make_async_remote_copy(
            src_ref=cols.at[kind, source],
            dst_ref=cols.at[kind, source],
            send_sem=mate_send.at[kind, step],
            recv_sem=mate_recv.at[kind, step],
            device_id=mate,
            device_id_type=MESH,
        )
        mate_copies[kind, step].start()

    def first_leg(kind):
        for step in NEAR[:2]:
            send_rows(kind, step, step)
        for step in (2, 3, 1):
            send_cols(kind, step)
        for step in NEAR[2:]:
            send_rows(kind, step, step)
        send_mate(kind, 0)

    def second_leg(kind):
        for sign in (1, -1):
            row_copies[kind, 2 * sign % col_count].wait_recv()
            if (sign == 1) == (kind == 0):
                send_rows(kind, 4 * sign, 2 * sign)
            send_rows(kind, 3 * sign, sign)

    def hand_over(kind):
        for step in (1, 2, 3):
            col_copies[kind, step].wait_recv()
            send_mate(kind, step)

    first_leg(0)

    def find(k, carry):
        slot = jnp.int32(0)
        for s in range(kpoints):
            slot = jnp.where(slot_kpoint[s] == k, s, slot)
        inverse[k] = slot
        return carry

    lax.fori_loop(0, kpoints, find, 0)
    twice = [jnp.concatenate([ref[...], ref[...]], axis=0) for ref in (levels, ranks)]
    weights = band_weights(*twice, imag_times)

    second_leg(0)
    first_leg(1)
    relay(1)
    hand_over(0)
    relay(2)
    relay(3)

    points = row_count * raw.shape[2]
    share = points // groups
    lanes = lax.broadcasted_iota(jnp.int32, (points, LANES), 1)
    for kind in range(2):
        if kind:
            second_leg(kind)
            hand_over(kind)
        for distance in (1, 7, 3, 5, 4):
            row_copies[kind, distance].wait_recv()
        for step in range(line):
            mate_copies[kind, step].wait_recv()
        powers = jnp.zeros((points, LANES), jnp.float32)
        for slot in range(per_group):
            row_panel = rows[kind, :, slot].reshape(-1, 2 * bands)
            col_panel = cols[kind, :, slot].reshape(-1, 2 * bands)
            at = kind * per_group + slot
            w = [weights[t][at : at + 1] for t in range(2)]
            wide = row_panel.astype(jnp.float32)
            scaled = jnp.concatenate(
                [wide * jnp.concatenate([w[t], w[t]], axis=1) for t in range(2)], axis=0
            ).astype(jnp.bfloat16)
            turned = jnp.concatenate([-col_panel[:, bands:], col_panel[:, :bands]], axis=1)
            stacked = jnp.concatenate([col_panel, turned], axis=0)
            tile = lax.dot_general(
                stacked, scaled, (((1,), (1,)), ((), ())), preferred_element_type=jnp.float32
            )
            for t in range(2):
                span = slice(t * LANES, (t + 1) * LANES)
                pair = [tile[:points, span], tile[points:, span]]
                largest = jnp.maximum(jnp.abs(pair[0]), jnp.abs(pair[1]))
                largest = jnp.maximum(jnp.max(largest, axis=1, keepdims=True), 1e-30)
                power = jnp.floor(jnp.log2(largest)) + 1.0
                unit = jnp.exp2(15.0 - power)
                powers = jnp.where(lanes == slot * 2 + t, power, powers)
                for comp in range(2):
                    value = jnp.clip(jnp.round(pair[comp] * unit), -TOP, TOP).astype(jnp.int16)
                    packed[kind, :, slot * 2 + t, comp * share : (comp + 1) * share] = (
                        value.reshape(groups, share, LANES)
                    )
        coded = powers.astype(jnp.int16).reshape(groups, share, LANES)
        for comp in range(2):
            packed[kind, :, 2 * per_group, comp * share : (comp + 1) * share] = coded
        for n, (dx, dz) in enumerate(others):
            there = group_at(dx, dz)
            tile_copies[kind, n] = pltpu.make_async_remote_copy(
                src_ref=packed.at[kind, there],
                dst_ref=landed.at[kind, group],
                send_sem=tile_send.at[kind, n],
                recv_sem=tile_recv.at[kind, n],
                device_id=(there, row, y),
                device_id_type=MESH,
            )
            tile_copies[kind, n].start()

    for copy in (*row_copies.values(), *col_copies.values(), *mate_copies.values()):
        copy.wait_send()

    def decode(kind, held, source):
        unit = jnp.exp2(held[kind, source, 2 * per_group].astype(jnp.float32) - 15.0)
        for slot in range(per_group):
            for t in range(2):
                k = slot * 2 + t
                value = held[kind, source, k].astype(jnp.float32) * unit[:, k : k + 1]
                decoded[kind, source * per_group + slot, t] = value

    for kind in range(2):
        decode(kind, packed, group)
        for n, (dx, dz) in reversed(list(enumerate(others))):
            tile_copies[kind, n].wait_recv()
            decode(kind, landed, group_at(-dx % xs, dz))

    def add(j, totals):
        held = decoded[0, j]
        held_re, held_im = held[:, :share], held[:, share:]
        kpoint = slot_kpoint[j]
        new = []
        for q in range(2):
            moved = decoded[1, inverse[kq_map[q, kpoint]]]
            moved_re, moved_im = moved[:, :share], moved[:, share:]
            new.append(totals[2 * q] + (held_re * moved_re + held_im * moved_im))
            new.append(totals[2 * q + 1] + (held_im * moved_re - held_re * moved_im))
        return tuple(new)

    zero = jnp.zeros((2, share, LANES), jnp.float32)
    totals = lax.fori_loop(0, kpoints, add, (zero,) * 4)
    for q in range(2):
        for comp in range(2):
            for t in range(2):
                out_ref[comp, q, 0, :, t, :] = totals[2 * q + comp][t]
    for copy in tile_copies.values():
        copy.wait_send()


def shards(sizes, occ, emp, energies, band_order, imag_times, kq_map, slot_kpoint):
    groups, row_count, col_count = sizes
    per_group, chunk, parts, bands = occ.shape
    width = parts * bands
    share = row_count * chunk // groups
    kpoints = groups * per_group
    dma = pltpu.SemaphoreType.DMA
    totals = pl.pallas_call(
        functools.partial(kernel, sizes),
        out_shape=jax.ShapeDtypeStruct((2, 2, 1, share, 2, col_count * chunk), jnp.float32),
        in_specs=[pl.BlockSpec(memory_space=pl.ANY)] * 7,
        out_specs=pl.BlockSpec(memory_space=pltpu.VMEM),
        scratch_shapes=[
            pltpu.VMEM((2, *occ.shape), jnp.bfloat16),
            pltpu.VMEM((2 * per_group, bands), jnp.float32),
            pltpu.VMEM((2 * per_group, bands), jnp.int32),
            pltpu.VMEM((2, col_count, per_group, chunk, width), jnp.bfloat16),
            pltpu.VMEM((2, row_count, per_group, chunk, width), jnp.bfloat16),
            pltpu.VMEM((2, groups, 2 * per_group + 1, 2 * share, LANES), jnp.int16),
            pltpu.VMEM((2, groups, 2 * per_group + 1, 2 * share, LANES), jnp.int16),
            pltpu.VMEM((2, kpoints, 2, 2 * share, LANES), jnp.float32),
            pltpu.SMEM(imag_times.shape, jnp.float32),
            pltpu.SMEM(kq_map.shape, jnp.int32),
            pltpu.SMEM(slot_kpoint.shape, jnp.int32),
            pltpu.SMEM((kpoints,), jnp.int32),
            dma((2, col_count)),
            dma((2, col_count)),
            dma((2, 4)),
            dma((2, 4)),
            dma((2, 4)),
            dma((2, 4)),
            dma((2, groups)),
            dma((2, groups)),
            dma((9,)),
            pltpu.SemaphoreType.REGULAR((len(RELAY),)),
        ],
        compiler_params=pltpu.CompilerParams(collective_id=0, has_side_effects=True),
        name="polarizability",
    )(occ, emp, energies, band_order, imag_times, kq_map, slot_kpoint)
    return totals * (-1.0 / kpoints)


def solution(mesh):
    sizes = (mesh.shape["kgrp"], mesh.shape["row"], mesh.shape["col"])
    in_specs = (
        P("kgrp", ("row", "col"), None, None),
        P("kgrp", ("row", "col"), None, None),
        P(),
        P(),
        P(),
        P(),
        P(),
    )
    out_specs = P(None, None, "col", "kgrp", None, "row")
    return jax.shard_map(
        functools.partial(shards, sizes),
        mesh=mesh,
        in_specs=in_specs,
        out_specs=out_specs,
        check_vma=False,
    )
```

```python
import functools

import jax
import jax.numpy as jnp
from jax import lax
from jax.experimental import pallas as pl
from jax.experimental.pallas import tpu as pltpu
from jax.sharding import PartitionSpec as P

MESH = pl.DeviceIdType.MESH
CORES = 2
LANES = 128
NEAR = (2, -2, 1, -1)
TOP = 32767.0
RELAY = ((1, -1), (2, -2), (1, -1))


def band_weights(levels, ranks, imag_times):
    pieces = levels.shape[1] // LANES
    picked = []
    for b in range(pieces):
        rank = ranks[:, b * LANES : (b + 1) * LANES]
        lane = rank % LANES
        found = jnp.zeros(rank.shape, jnp.float32)
        for c in range(pieces):
            taken = jnp.take_along_axis(levels[:, c * LANES : (c + 1) * LANES], lane, axis=1)
            found = jnp.where(rank // LANES == c, taken, found)
        picked.append(found)
    picked = jnp.concatenate(picked, axis=1)
    return [jnp.exp(-picked * imag_times[t]) for t in range(2)]


def kernel(
    sizes,
    occ_hbm,
    emp_hbm,
    energies_hbm,
    order_hbm,
    times_hbm,
    kq_hbm,
    kpoint_hbm,
    out_ref,
    raw,
    levels,
    ranks,
    rows,
    cols,
    packed,
    landed,
    decoded,
    imag_times,
    kq_map,
    slot_kpoint,
    inverse,
    row_send,
    row_recv,
    col_send,
    col_recv,
    mate_send,
    mate_recv,
    tile_send,
    tile_recv,
    local_sem,
    relay_sem,
):
    groups, row_count, col_count = sizes
    xs, line = groups // 2, row_count // CORES
    per_group = raw.shape[1]
    bands = raw.shape[4]
    kpoints = groups * per_group
    group, row, y = lax.axis_index("kgrp"), lax.axis_index("row"), lax.axis_index("col")
    x, zh = group // 2, group % 2
    zl, core = row // CORES, row % CORES

    def along_y(step):
        return (group, row, lax.rem(y + step + col_count, col_count))

    def along_z(step):
        return (group, lax.rem(zl + step, line) * CORES + core, y)

    mate = (group, zl * CORES + 1 - core, y)
    others = [(dx, dz) for dx in (4, 3, 5, 2, 6, 1, 7, 0) for dz in (1, 0) if dx or dz]

    def group_at(dx, dz):
        return lax.rem(x + dx, xs) * 2 + lax.rem(zh + dz, 2)

    def along_x(dx, dz=0):
        return (group_at(dx % xs, dz), row, y)

    peers = [along_x(0, 1), along_x(1), along_x(-1)]
    peers += [along_z(e) for e in range(1, line)] + [along_y(s) for s in NEAR] + [mate]
    barrier = pltpu.get_barrier_semaphore()
    for peer in peers:
        pl.semaphore_signal(barrier, inc=1, device_id=peer, device_id_type=MESH)

    own = pl.ds(group * per_group, per_group)
    fetches = [
        pltpu.make_async_copy(occ_hbm, raw.at[0], local_sem.at[0]),
        pltpu.make_async_copy(emp_hbm, raw.at[1], local_sem.at[1]),
        pltpu.make_async_copy(times_hbm, imag_times, local_sem.at[2]),
        pltpu.make_async_copy(kq_hbm, kq_map, local_sem.at[3]),
        pltpu.make_async_copy(kpoint_hbm, slot_kpoint, local_sem.at[4]),
    ]
    for kind in range(2):
        part = pl.ds(kind * per_group, per_group)
        fetches += [
            pltpu.make_async_copy(
                energies_hbm.at[kind, own], levels.at[part], local_sem.at[5 + kind]
            ),
            pltpu.make_async_copy(order_hbm.at[kind, own], ranks.at[part], local_sem.at[7 + kind]),
        ]
    for copy in fetches:
        copy.start()
    for copy in fetches:
        copy.wait()
    for kind in range(2):
        for slot in range(per_group):
            for part in range(2):
                piece = raw[kind, slot, :, part, :]
                span = slice(part * bands, (part + 1) * bands)
                rows[kind, y, slot, :, span] = piece
                cols[kind, row, slot, :, span] = piece

    pl.semaphore_wait(barrier, len(peers))

    def relay(stage):
        if stage:
            pl.semaphore_wait(relay_sem.at[stage - 1], len(RELAY[stage - 1]))
        if stage < len(RELAY):
            for dx in RELAY[stage]:
                pl.semaphore_signal(
                    relay_sem.at[stage], inc=1, device_id=along_x(dx), device_id_type=MESH
                )

    relay(0)

    row_copies, col_copies, mate_copies, tile_copies = {}, {}, {}, {}

    def send_rows(kind, distance, step):
        source = lax.rem(y - (distance - step) + col_count, col_count)
        key = (kind, distance % col_count)
        row_copies[key] = pltpu.make_async_remote_copy(
            src_ref=rows.at[kind, source],
            dst_ref=rows.at[kind, source],
            send_sem=row_send.at[key[0], key[1]],
            recv_sem=row_recv.at[key[0], key[1]],
            device_id=along_y(step),
            device_id_type=MESH,
        )
        row_copies[key].start()

    def send_cols(kind, step):
        col_copies[kind, step] = pltpu.make_async_remote_copy(
            src_ref=cols.at[kind, row],
            dst_ref=cols.at[kind, row],
            send_sem=col_send.at[kind, step],
            recv_sem=col_recv.at[kind, step],
            device_id=along_z(step),
            device_id_type=MESH,
        )
        col_copies[kind, step].start()

    def send_mate(kind, step):
        source = lax.rem(zl - step + line, line) * CORES + core
        mate_copies[kind, step] = pltpu.make_async_remote_copy(
            src_ref=cols.at[kind, source],
            dst_ref=cols.at[kind, source],
            send_sem=mate_send.at[kind, step],
            recv_sem=mate_recv.at[kind, step],
            device_id=mate,
            device_id_type=MESH,
        )
        mate_copies[kind, step].start()

    def first_leg(kind):
        for step in NEAR[:2]:
            send_rows(kind, step, step)
        for step in (2, 3, 1):
            send_cols(kind, step)
        for step in NEAR[2:]:
            send_rows(kind, step, step)
        send_mate(kind, 0)

    def second_leg(kind):
        for sign in (1, -1):
            row_copies[kind, 2 * sign % col_count].wait_recv()
            if (sign == 1) == (kind == 0):
                send_rows(kind, 4 * sign, 2 * sign)
            send_rows(kind, 3 * sign, sign)

    def hand_over(kind):
        for step in (1, 2, 3):
            col_copies[kind, step].wait_recv()
            send_mate(kind, step)

    first_leg(0)

    def find(k, carry):
        slot = jnp.int32(0)
        for s in range(kpoints):
            slot = jnp.where(slot_kpoint[s] == k, s, slot)
        inverse[k] = slot
        return carry

    lax.fori_loop(0, kpoints, find, 0)
    twice = [jnp.concatenate([ref[...], ref[...]], axis=0) for ref in (levels, ranks)]
    weights = band_weights(*twice, imag_times)

    second_leg(0)
    first_leg(1)
    relay(1)
    hand_over(0)
    relay(2)
    relay(3)

    points = row_count * raw.shape[2]
    share = points // groups
    lanes = lax.broadcasted_iota(jnp.int32, (points, LANES), 1)
    powers = jnp.zeros((points, LANES), jnp.float32)
    for kind in range(2):
        if kind:
            second_leg(kind)
            hand_over(kind)
        for distance in (1, 7, 3, 5, 4):
            row_copies[kind, distance].wait_recv()
        for step in range(line):
            mate_copies[kind, step].wait_recv()
        for slot in range(per_group):
            row_panel = rows[kind, :, slot].reshape(-1, 2 * bands)
            col_panel = cols[kind, :, slot].reshape(-1, 2 * bands)
            at = kind * per_group + slot
            w = [weights[t][at : at + 1] for t in range(2)]
            wide = row_panel.astype(jnp.float32)
            scaled = jnp.concatenate(
                [wide * jnp.concatenate([w[t], w[t]], axis=1) for t in range(2)], axis=0
            ).astype(jnp.bfloat16)
            turned = jnp.concatenate([-col_panel[:, bands:], col_panel[:, :bands]], axis=1)
            stacked = jnp.concatenate([col_panel, turned], axis=0)
            tile = lax.dot_general(
                stacked, scaled, (((1,), (1,)), ((), ())), preferred_element_type=jnp.float32
            )
            for t in range(2):
                span = slice(t * LANES, (t + 1) * LANES)
                pair = [tile[:points, span], tile[points:, span]]
                largest = jnp.maximum(jnp.abs(pair[0]), jnp.abs(pair[1]))
                largest = jnp.maximum(jnp.max(largest, axis=1, keepdims=True), 1e-30)
                power = jnp.floor(jnp.log2(largest)) + 1.0
                unit = jnp.exp2(15.0 - power)
                powers = jnp.where(lanes == at * 2 + t, power, powers)
                for comp in range(2):
                    value = jnp.clip(jnp.round(pair[comp] * unit), -TOP, TOP).astype(jnp.int16)
                    packed[kind, :, slot * 2 + t, comp * share : (comp + 1) * share] = (
                        value.reshape(groups, share, LANES)
                    )
        count = 2 * per_group + kind
        if kind:
            coded = powers.astype(jnp.int16).reshape(groups, share, LANES)
            for comp in range(2):
                span = slice(comp * share, (comp + 1) * share)
                packed[kind, :, 2 * per_group, span] = coded
        for n, (dx, dz) in enumerate(others):
            there = group_at(dx, dz)
            tile_copies[kind, n] = pltpu.make_async_remote_copy(
                src_ref=packed.at[kind, there, pl.ds(0, count)],
                dst_ref=landed.at[kind, group, pl.ds(0, count)],
                send_sem=tile_send.at[kind, n],
                recv_sem=tile_recv.at[kind, n],
                device_id=(there, row, y),
                device_id_type=MESH,
            )
            tile_copies[kind, n].start()

    for copy in (*row_copies.values(), *col_copies.values(), *mate_copies.values()):
        copy.wait_send()

    def decode(held, source):
        unit = jnp.exp2(held[1, source, 2 * per_group].astype(jnp.float32) - 15.0)
        for kind in range(2):
            for slot in range(per_group):
                for t in range(2):
                    k = slot * 2 + t
                    at = kind * per_group * 2 + k
                    value = held[kind, source, k].astype(jnp.float32) * unit[:, at : at + 1]
                    decoded[kind, source * per_group + slot, t] = value

    decode(packed, group)
    for n, (dx, dz) in reversed(list(enumerate(others))):
        for kind in range(2):
            tile_copies[kind, n].wait_recv()
        decode(landed, group_at(-dx % xs, dz))

    def add(j, totals):
        held = decoded[0, j]
        held_re, held_im = held[:, :share], held[:, share:]
        kpoint = slot_kpoint[j]
        new = []
        for q in range(2):
            moved = decoded[1, inverse[kq_map[q, kpoint]]]
            moved_re, moved_im = moved[:, :share], moved[:, share:]
            new.append(totals[2 * q] + (held_re * moved_re + held_im * moved_im))
            new.append(totals[2 * q + 1] + (held_im * moved_re - held_re * moved_im))
        return tuple(new)

    zero = jnp.zeros((2, share, LANES), jnp.float32)
    totals = lax.fori_loop(0, kpoints, add, (zero,) * 4)
    for q in range(2):
        for comp in range(2):
            for t in range(2):
                out_ref[comp, q, 0, :, t, :] = totals[2 * q + comp][t]
    for copy in tile_copies.values():
        copy.wait_send()


def shards(sizes, occ, emp, energies, band_order, imag_times, kq_map, slot_kpoint):
    groups, row_count, col_count = sizes
    per_group, chunk, parts, bands = occ.shape
    width = parts * bands
    share = row_count * chunk // groups
    kpoints = groups * per_group
    dma = pltpu.SemaphoreType.DMA
    totals = pl.pallas_call(
        functools.partial(kernel, sizes),
        out_shape=pltpu.VMEM((2, 2, 1, share, 2, col_count * chunk), jnp.float32),
        in_specs=[pl.BlockSpec(memory_space=pl.ANY)] * 7,
        out_specs=pl.BlockSpec(memory_space=pltpu.VMEM),
        scratch_shapes=[
            pltpu.VMEM((2, *occ.shape), jnp.bfloat16),
            pltpu.VMEM((2 * per_group, bands), jnp.float32),
            pltpu.VMEM((2 * per_group, bands), jnp.int32),
            pltpu.VMEM((2, col_count, per_group, chunk, width), jnp.bfloat16),
            pltpu.VMEM((2, row_count, per_group, chunk, width), jnp.bfloat16),
            pltpu.VMEM((2, groups, 2 * per_group + 1, 2 * share, LANES), jnp.int16),
            pltpu.VMEM((2, groups, 2 * per_group + 1, 2 * share, LANES), jnp.int16),
            pltpu.VMEM((2, kpoints, 2, 2 * share, LANES), jnp.float32),
            pltpu.SMEM(imag_times.shape, jnp.float32),
            pltpu.SMEM(kq_map.shape, jnp.int32),
            pltpu.SMEM(slot_kpoint.shape, jnp.int32),
            pltpu.SMEM((kpoints,), jnp.int32),
            dma((2, col_count)),
            dma((2, col_count)),
            dma((2, 4)),
            dma((2, 4)),
            dma((2, 4)),
            dma((2, 4)),
            dma((2, groups)),
            dma((2, groups)),
            dma((9,)),
            pltpu.SemaphoreType.REGULAR((len(RELAY),)),
        ],
        compiler_params=pltpu.CompilerParams(collective_id=0, has_side_effects=True),
        name="polarizability",
    )(occ, emp, energies, band_order, imag_times, kq_map, slot_kpoint)
    return totals * (-1.0 / kpoints)


def solution(mesh):
    sizes = (mesh.shape["kgrp"], mesh.shape["row"], mesh.shape["col"])
    in_specs = (
        P("kgrp", ("row", "col"), None, None),
        P("kgrp", ("row", "col"), None, None),
        P(),
        P(),
        P(),
        P(),
        P(),
    )
    out_specs = P(None, None, "col", "kgrp", None, "row")
    return jax.shard_map(
        functools.partial(shards, sizes),
        mesh=mesh,
        in_specs=in_specs,
        out_specs=out_specs,
        check_vma=False,
    )
```

```python
import functools

import jax
import jax.numpy as jnp
from jax import lax
from jax.experimental import pallas as pl
from jax.experimental.pallas import tpu as pltpu
from jax.sharding import PartitionSpec as P

MESH = pl.DeviceIdType.MESH
CORES = 2
LANES = 128
UNROLL = 4
NEAR = (2, -2, 1, -1)
TOP = 32767.0
RELAY = ((1, -1), (2, -2), (1, -1))


def band_weights(levels, ranks, imag_times):
    pieces = levels.shape[1] // LANES
    picked = []
    for b in range(pieces):
        rank = ranks[:, b * LANES : (b + 1) * LANES]
        lane = rank % LANES
        found = jnp.zeros(rank.shape, jnp.float32)
        for c in range(pieces):
            taken = jnp.take_along_axis(levels[:, c * LANES : (c + 1) * LANES], lane, axis=1)
            found = jnp.where(rank // LANES == c, taken, found)
        picked.append(found)
    picked = jnp.concatenate(picked, axis=1)
    return [jnp.exp(-picked * imag_times[t]) for t in range(2)]


def kernel(
    sizes,
    occ_hbm,
    emp_hbm,
    energies_hbm,
    order_hbm,
    times_hbm,
    kq_hbm,
    kpoint_hbm,
    out_ref,
    raw,
    levels,
    ranks,
    rows,
    cols,
    packed,
    landed,
    decoded,
    imag_times,
    kq_map,
    slot_kpoint,
    inverse,
    sources,
    row_send,
    row_recv,
    col_send,
    col_recv,
    mate_send,
    mate_recv,
    tile_send,
    tile_recv,
    local_sem,
    relay_sem,
):
    groups, row_count, col_count = sizes
    xs, line = groups // 2, row_count // CORES
    per_group = raw.shape[1]
    bands = raw.shape[4]
    kpoints = groups * per_group
    group, row, y = lax.axis_index("kgrp"), lax.axis_index("row"), lax.axis_index("col")
    x, zh = group // 2, group % 2
    zl, core = row // CORES, row % CORES

    def along_y(step):
        return (group, row, lax.rem(y + step + col_count, col_count))

    def along_z(step):
        return (group, lax.rem(zl + step, line) * CORES + core, y)

    mate = (group, zl * CORES + 1 - core, y)
    others = [(dx, dz) for dx in (4, 3, 5, 2, 6, 1, 7, 0) for dz in (1, 0) if dx or dz]

    def group_at(dx, dz):
        return lax.rem(x + dx, xs) * 2 + lax.rem(zh + dz, 2)

    def along_x(dx, dz=0):
        return (group_at(dx % xs, dz), row, y)

    peers = [along_x(0, 1), along_x(1), along_x(-1)]
    peers += [along_z(e) for e in range(1, line)] + [along_y(s) for s in NEAR] + [mate]
    barrier = pltpu.get_barrier_semaphore()
    for peer in peers:
        pl.semaphore_signal(barrier, inc=1, device_id=peer, device_id_type=MESH)

    own = pl.ds(group * per_group, per_group)
    fetches = [
        pltpu.make_async_copy(occ_hbm, raw.at[0], local_sem.at[0]),
        pltpu.make_async_copy(emp_hbm, raw.at[1], local_sem.at[1]),
        pltpu.make_async_copy(times_hbm, imag_times, local_sem.at[2]),
        pltpu.make_async_copy(kq_hbm, kq_map, local_sem.at[3]),
        pltpu.make_async_copy(kpoint_hbm, slot_kpoint, local_sem.at[4]),
    ]
    for kind in range(2):
        part = pl.ds(kind * per_group, per_group)
        fetches += [
            pltpu.make_async_copy(
                energies_hbm.at[kind, own], levels.at[part], local_sem.at[5 + kind]
            ),
            pltpu.make_async_copy(order_hbm.at[kind, own], ranks.at[part], local_sem.at[7 + kind]),
        ]
    for copy in fetches:
        copy.start()
    for copy in fetches:
        copy.wait()
    for kind in range(2):
        for slot in range(per_group):
            for part in range(2):
                piece = raw[kind, slot, :, part, :]
                span = slice(part * bands, (part + 1) * bands)
                rows[kind, y, slot, :, span] = piece
                cols[kind, row, slot, :, span] = piece

    twice = [jnp.concatenate([ref[...], ref[...]], axis=0) for ref in (levels, ranks)]
    weights = band_weights(*twice, imag_times)

    pl.semaphore_wait(barrier, len(peers))

    def relay(stage):
        if stage:
            pl.semaphore_wait(relay_sem.at[stage - 1], len(RELAY[stage - 1]))
        if stage < len(RELAY):
            for dx in RELAY[stage]:
                pl.semaphore_signal(
                    relay_sem.at[stage], inc=1, device_id=along_x(dx), device_id_type=MESH
                )

    relay(0)

    row_copies, col_copies, mate_copies, tile_copies = {}, {}, {}, {}

    def send_rows(kind, distance, step):
        source = lax.rem(y - (distance - step) + col_count, col_count)
        key = (kind, distance % col_count)
        row_copies[key] = pltpu.make_async_remote_copy(
            src_ref=rows.at[kind, source],
            dst_ref=rows.at[kind, source],
            send_sem=row_send.at[key[0], key[1]],
            recv_sem=row_recv.at[key[0], key[1]],
            device_id=along_y(step),
            device_id_type=MESH,
        )
        row_copies[key].start()

    def send_cols(kind, step):
        col_copies[kind, step] = pltpu.make_async_remote_copy(
            src_ref=cols.at[kind, row],
            dst_ref=cols.at[kind, row],
            send_sem=col_send.at[kind, step],
            recv_sem=col_recv.at[kind, step],
            device_id=along_z(step),
            device_id_type=MESH,
        )
        col_copies[kind, step].start()

    def send_mate(kind, step):
        source = lax.rem(zl - step + line, line) * CORES + core
        mate_copies[kind, step] = pltpu.make_async_remote_copy(
            src_ref=cols.at[kind, source],
            dst_ref=cols.at[kind, source],
            send_sem=mate_send.at[kind, step],
            recv_sem=mate_recv.at[kind, step],
            device_id=mate,
            device_id_type=MESH,
        )
        mate_copies[kind, step].start()

    def first_leg(kind):
        for step in NEAR[:2]:
            send_rows(kind, step, step)
        for step in (2, 3, 1):
            send_cols(kind, step)
        for step in NEAR[2:]:
            send_rows(kind, step, step)
        send_mate(kind, 0)

    def second_leg(kind):
        for sign in (1, -1):
            row_copies[kind, 2 * sign % col_count].wait_recv()
            if (sign == 1) == (kind == 0):
                send_rows(kind, 4 * sign, 2 * sign)
            send_rows(kind, 3 * sign, sign)

    def hand_over(kind):
        for step in (1, 2, 3):
            col_copies[kind, step].wait_recv()
            send_mate(kind, step)

    first_leg(0)

    def find(k, carry):
        slot = jnp.int32(0)
        for s in range(kpoints):
            slot = jnp.where(slot_kpoint[s] == k, s, slot)
        inverse[k] = slot
        return carry

    def look_up(j, carry):
        for q in range(2):
            sources[q, j] = inverse[kq_map[q, slot_kpoint[j]]]
        return carry

    lax.fori_loop(0, kpoints, find, 0)

    second_leg(0)
    first_leg(1)
    relay(1)
    hand_over(0)
    relay(2)
    relay(3)

    points = row_count * raw.shape[2]
    share = points // groups
    lanes = lax.broadcasted_iota(jnp.int32, (points, LANES), 1)
    powers = jnp.zeros((points, LANES), jnp.float32)
    for kind in range(2):
        if kind:
            second_leg(kind)
            hand_over(kind)
        for distance in (1, 7, 3, 5, 4):
            row_copies[kind, distance].wait_recv()
        for step in range(line):
            mate_copies[kind, step].wait_recv()
        for slot in range(per_group):
            row_panel = rows[kind, :, slot].reshape(-1, 2 * bands)
            col_panel = cols[kind, :, slot].reshape(-1, 2 * bands)
            at = kind * per_group + slot
            w = [weights[t][at : at + 1] for t in range(2)]
            wide = row_panel.astype(jnp.float32)
            scaled = jnp.concatenate(
                [wide * jnp.concatenate([w[t], w[t]], axis=1) for t in range(2)], axis=0
            ).astype(jnp.bfloat16)
            turned = jnp.concatenate([-col_panel[:, bands:], col_panel[:, :bands]], axis=1)
            stacked = jnp.concatenate([col_panel, turned], axis=0)
            tile = lax.dot_general(
                stacked, scaled, (((1,), (1,)), ((), ())), preferred_element_type=jnp.float32
            )
            for t in range(2):
                span = slice(t * LANES, (t + 1) * LANES)
                pair = [tile[:points, span], tile[points:, span]]
                largest = jnp.maximum(jnp.abs(pair[0]), jnp.abs(pair[1]))
                largest = jnp.maximum(jnp.max(largest, axis=1, keepdims=True), 1e-30)
                power = jnp.floor(jnp.log2(largest)) + 1.0
                unit = jnp.exp2(15.0 - power)
                powers = jnp.where(lanes == at * 2 + t, power, powers)
                for comp in range(2):
                    value = jnp.clip(jnp.round(pair[comp] * unit), -TOP, TOP).astype(jnp.int16)
                    packed[kind, :, slot * 2 + t, comp * share : (comp + 1) * share] = (
                        value.reshape(groups, share, LANES)
                    )
        count = 2 * per_group + kind
        if kind:
            coded = powers.astype(jnp.int16).reshape(groups, share, LANES)
            for comp in range(2):
                span = slice(comp * share, (comp + 1) * share)
                packed[kind, :, 2 * per_group, span] = coded
        for n, (dx, dz) in enumerate(others):
            there = group_at(dx, dz)
            tile_copies[kind, n] = pltpu.make_async_remote_copy(
                src_ref=packed.at[kind, there, pl.ds(0, count)],
                dst_ref=landed.at[kind, group, pl.ds(0, count)],
                send_sem=tile_send.at[kind, n],
                recv_sem=tile_recv.at[kind, n],
                device_id=(there, row, y),
                device_id_type=MESH,
            )
            tile_copies[kind, n].start()

    for copy in (*row_copies.values(), *col_copies.values(), *mate_copies.values()):
        copy.wait_send()

    lax.fori_loop(0, kpoints, look_up, 0)

    def decode(held, source):
        unit = jnp.exp2(held[1, source, 2 * per_group].astype(jnp.float32) - 15.0)
        for kind in range(2):
            for slot in range(per_group):
                for t in range(2):
                    k = slot * 2 + t
                    at = kind * per_group * 2 + k
                    value = held[kind, source, k].astype(jnp.float32) * unit[:, at : at + 1]
                    decoded[kind, source * per_group + slot, t] = value

    decode(packed, group)
    for n, (dx, dz) in reversed(list(enumerate(others))):
        for kind in range(2):
            tile_copies[kind, n].wait_recv()
        decode(landed, group_at(-dx % xs, dz))

    def add(step, totals):
        for part in range(UNROLL):
            j = step * UNROLL + part
            held = decoded[0, j]
            held_re, held_im = held[:, :share], held[:, share:]
            new = []
            for q in range(2):
                moved = decoded[1, sources[q, j]]
                moved_re, moved_im = moved[:, :share], moved[:, share:]
                new.append(totals[2 * q] + (held_re * moved_re + held_im * moved_im))
                new.append(totals[2 * q + 1] + (held_im * moved_re - held_re * moved_im))
            totals = tuple(new)
        return totals

    zero = jnp.zeros((2, share, LANES), jnp.float32)
    totals = lax.fori_loop(0, kpoints // UNROLL, add, (zero,) * 4)
    for q in range(2):
        for comp in range(2):
            for t in range(2):
                out_ref[comp, q, 0, :, t, :] = totals[2 * q + comp][t]
    for copy in tile_copies.values():
        copy.wait_send()


def shards(sizes, occ, emp, energies, band_order, imag_times, kq_map, slot_kpoint):
    groups, row_count, col_count = sizes
    per_group, chunk, parts, bands = occ.shape
    width = parts * bands
    share = row_count * chunk // groups
    kpoints = groups * per_group
    dma = pltpu.SemaphoreType.DMA
    totals = pl.pallas_call(
        functools.partial(kernel, sizes),
        out_shape=pltpu.VMEM((2, 2, 1, share, 2, col_count * chunk), jnp.float32),
        in_specs=[pl.BlockSpec(memory_space=pl.ANY)] * 7,
        out_specs=pl.BlockSpec(memory_space=pltpu.VMEM),
        scratch_shapes=[
            pltpu.VMEM((2, *occ.shape), jnp.bfloat16),
            pltpu.VMEM((2 * per_group, bands), jnp.float32),
            pltpu.VMEM((2 * per_group, bands), jnp.int32),
            pltpu.VMEM((2, col_count, per_group, chunk, width), jnp.bfloat16),
            pltpu.VMEM((2, row_count, per_group, chunk, width), jnp.bfloat16),
            pltpu.VMEM((2, groups, 2 * per_group + 1, 2 * share, LANES), jnp.int16),
            pltpu.VMEM((2, groups, 2 * per_group + 1, 2 * share, LANES), jnp.int16),
            pltpu.VMEM((2, kpoints, 2, 2 * share, LANES), jnp.float32),
            pltpu.SMEM(imag_times.shape, jnp.float32),
            pltpu.SMEM(kq_map.shape, jnp.int32),
            pltpu.SMEM(slot_kpoint.shape, jnp.int32),
            pltpu.SMEM((kpoints,), jnp.int32),
            pltpu.SMEM((2, kpoints), jnp.int32),
            dma((2, col_count)),
            dma((2, col_count)),
            dma((2, 4)),
            dma((2, 4)),
            dma((2, 4)),
            dma((2, 4)),
            dma((2, groups)),
            dma((2, groups)),
            dma((9,)),
            pltpu.SemaphoreType.REGULAR((len(RELAY),)),
        ],
        compiler_params=pltpu.CompilerParams(collective_id=0, has_side_effects=True),
        name="polarizability",
    )(occ, emp, energies, band_order, imag_times, kq_map, slot_kpoint)
    return totals * (-1.0 / kpoints)


def solution(mesh):
    sizes = (mesh.shape["kgrp"], mesh.shape["row"], mesh.shape["col"])
    in_specs = (
        P("kgrp", ("row", "col"), None, None),
        P("kgrp", ("row", "col"), None, None),
        P(),
        P(),
        P(),
        P(),
        P(),
    )
    out_specs = P(None, None, "col", "kgrp", None, "row")
    return jax.shard_map(
        functools.partial(shards, sizes),
        mesh=mesh,
        in_specs=in_specs,
        out_specs=out_specs,
        check_vma=False,
    )
```

```python
import functools

import jax
import jax.numpy as jnp
from jax import lax
from jax.experimental import pallas as pl
from jax.experimental.pallas import tpu as pltpu
from jax.sharding import PartitionSpec as P

MESH = pl.DeviceIdType.MESH
CORES = 2
LANES = 128
UNROLL = 4
NEAR = (2, -2, 1, -1)
TOP = 32767.0
RELAY = ((1, -1), (2, -2), (1, -1))


def band_weights(levels, ranks, imag_times):
    pieces = levels.shape[1] // LANES
    picked = []
    for b in range(pieces):
        rank = ranks[:, b * LANES : (b + 1) * LANES]
        lane = rank % LANES
        found = jnp.zeros(rank.shape, jnp.float32)
        for c in range(pieces):
            taken = jnp.take_along_axis(levels[:, c * LANES : (c + 1) * LANES], lane, axis=1)
            found = jnp.where(rank // LANES == c, taken, found)
        picked.append(found)
    picked = jnp.concatenate(picked, axis=1)
    return [jnp.exp(-picked * imag_times[t]) for t in range(2)]


def kernel(
    sizes,
    occ_hbm,
    emp_hbm,
    energies_hbm,
    order_hbm,
    times_hbm,
    kq_hbm,
    kpoint_hbm,
    out_ref,
    raw,
    levels,
    ranks,
    rows,
    cols,
    packed,
    landed,
    decoded,
    imag_times,
    kq_map,
    slot_kpoint,
    inverse,
    sources,
    row_send,
    row_recv,
    col_send,
    col_recv,
    mate_send,
    mate_recv,
    tile_send,
    tile_recv,
    local_sem,
    relay_sem,
):
    groups, row_count, col_count = sizes
    xs, line = groups // 2, row_count // CORES
    per_group = raw.shape[1]
    bands = raw.shape[4]
    kpoints = groups * per_group
    group, row, y = lax.axis_index("kgrp"), lax.axis_index("row"), lax.axis_index("col")
    x, zh = group // 2, group % 2
    zl, core = row // CORES, row % CORES

    def along_y(step):
        return (group, row, lax.rem(y + step + col_count, col_count))

    def along_z(step):
        return (group, lax.rem(zl + step, line) * CORES + core, y)

    mate = (group, zl * CORES + 1 - core, y)
    others = [(dx, dz) for dx in (4, 3, 5, 2, 6, 1, 7, 0) for dz in (1, 0) if dx or dz]

    def group_at(dx, dz):
        return lax.rem(x + dx, xs) * 2 + lax.rem(zh + dz, 2)

    def along_x(dx, dz=0):
        return (group_at(dx % xs, dz), row, y)

    peers = [along_x(0, 1), along_x(1), along_x(-1)]
    peers += [along_z(e) for e in range(1, line)] + [along_y(s) for s in NEAR] + [mate]
    barrier = pltpu.get_barrier_semaphore()
    for peer in peers:
        pl.semaphore_signal(barrier, inc=1, device_id=peer, device_id_type=MESH)

    own = pl.ds(group * per_group, per_group)
    fetches = [
        pltpu.make_async_copy(occ_hbm, raw.at[0], local_sem.at[0]),
        pltpu.make_async_copy(emp_hbm, raw.at[1], local_sem.at[1]),
        pltpu.make_async_copy(times_hbm, imag_times, local_sem.at[2]),
        pltpu.make_async_copy(kq_hbm, kq_map, local_sem.at[3]),
        pltpu.make_async_copy(kpoint_hbm, slot_kpoint, local_sem.at[4]),
    ]
    for kind in range(2):
        part = pl.ds(kind * per_group, per_group)
        fetches += [
            pltpu.make_async_copy(
                energies_hbm.at[kind, own], levels.at[part], local_sem.at[5 + kind]
            ),
            pltpu.make_async_copy(order_hbm.at[kind, own], ranks.at[part], local_sem.at[7 + kind]),
        ]
    for copy in fetches:
        copy.start()
    for copy in fetches:
        copy.wait()
    for kind in range(2):
        for slot in range(per_group):
            for part in range(2):
                piece = raw[kind, slot, :, part, :]
                span = slice(part * bands, (part + 1) * bands)
                rows[kind, y, slot, :, span] = piece
                cols[kind, row, slot, :, span] = piece

    twice = [jnp.concatenate([ref[...], ref[...]], axis=0) for ref in (levels, ranks)]
    weights = band_weights(*twice, imag_times)

    pl.semaphore_wait(barrier, len(peers))

    def relay(stage):
        if stage:
            pl.semaphore_wait(relay_sem.at[stage - 1], len(RELAY[stage - 1]))
        if stage < len(RELAY):
            for dx in RELAY[stage]:
                pl.semaphore_signal(
                    relay_sem.at[stage], inc=1, device_id=along_x(dx), device_id_type=MESH
                )

    relay(0)

    row_copies, col_copies, mate_copies, tile_copies = {}, {}, {}, {}

    def send_rows(kind, distance, step):
        source = lax.rem(y - (distance - step) + col_count, col_count)
        key = (kind, distance % col_count)
        row_copies[key] = pltpu.make_async_remote_copy(
            src_ref=rows.at[kind, source],
            dst_ref=rows.at[kind, source],
            send_sem=row_send.at[key[0], key[1]],
            recv_sem=row_recv.at[key[0], key[1]],
            device_id=along_y(step),
            device_id_type=MESH,
        )
        row_copies[key].start()

    def send_half(kind, sign):
        source = lax.rem(y - 2 * sign + col_count, col_count)
        slot, at = (0, 4) if sign == 1 else (1, 0)
        row_copies[kind, at] = pltpu.make_async_remote_copy(
            src_ref=rows.at[kind, source, slot],
            dst_ref=rows.at[kind, source, slot],
            send_sem=row_send.at[kind, at],
            recv_sem=row_recv.at[kind, at],
            device_id=along_y(2 * sign),
            device_id_type=MESH,
        )
        row_copies[kind, at].start()

    def send_cols(kind, step):
        col_copies[kind, step] = pltpu.make_async_remote_copy(
            src_ref=cols.at[kind, row],
            dst_ref=cols.at[kind, row],
            send_sem=col_send.at[kind, step],
            recv_sem=col_recv.at[kind, step],
            device_id=along_z(step),
            device_id_type=MESH,
        )
        col_copies[kind, step].start()

    def send_mate(kind, step):
        source = lax.rem(zl - step + line, line) * CORES + core
        mate_copies[kind, step] = pltpu.make_async_remote_copy(
            src_ref=cols.at[kind, source],
            dst_ref=cols.at[kind, source],
            send_sem=mate_send.at[kind, step],
            recv_sem=mate_recv.at[kind, step],
            device_id=mate,
            device_id_type=MESH,
        )
        mate_copies[kind, step].start()

    def first_leg(kind):
        for step in NEAR[:2]:
            send_rows(kind, step, step)
        for step in (2, 3, 1):
            send_cols(kind, step)
        for step in NEAR[2:]:
            send_rows(kind, step, step)
        send_mate(kind, 0)

    def second_leg(kind):
        for sign in (1, -1):
            row_copies[kind, 2 * sign % col_count].wait_recv()
            send_rows(kind, 3 * sign, sign)
            send_half(kind, sign)

    def hand_over(kind):
        for step in (1, 2, 3):
            col_copies[kind, step].wait_recv()
            send_mate(kind, step)

    first_leg(0)

    def find(k, carry):
        slot = jnp.int32(0)
        for s in range(kpoints):
            slot = jnp.where(slot_kpoint[s] == k, s, slot)
        inverse[k] = slot
        return carry

    def look_up(j, carry):
        for q in range(2):
            sources[q, j] = inverse[kq_map[q, slot_kpoint[j]]]
        return carry

    lax.fori_loop(0, kpoints, find, 0)

    second_leg(0)
    first_leg(1)
    relay(1)
    hand_over(0)
    relay(2)
    relay(3)

    points = row_count * raw.shape[2]
    share = points // groups
    lanes = lax.broadcasted_iota(jnp.int32, (points, LANES), 1)
    powers = jnp.zeros((points, LANES), jnp.float32)
    for kind in range(2):
        if kind:
            second_leg(kind)
            hand_over(kind)
        for distance in (1, 7, 3, 5, 4, 0):
            row_copies[kind, distance].wait_recv()
        for step in range(line):
            mate_copies[kind, step].wait_recv()
        for slot in range(per_group):
            row_panel = rows[kind, :, slot].reshape(-1, 2 * bands)
            col_panel = cols[kind, :, slot].reshape(-1, 2 * bands)
            at = kind * per_group + slot
            w = [weights[t][at : at + 1] for t in range(2)]
            wide = row_panel.astype(jnp.float32)
            scaled = jnp.concatenate(
                [wide * jnp.concatenate([w[t], w[t]], axis=1) for t in range(2)], axis=0
            ).astype(jnp.bfloat16)
            turned = jnp.concatenate([-col_panel[:, bands:], col_panel[:, :bands]], axis=1)
            stacked = jnp.concatenate([col_panel, turned], axis=0)
            tile = lax.dot_general(
                stacked, scaled, (((1,), (1,)), ((), ())), preferred_element_type=jnp.float32
            )
            for t in range(2):
                span = slice(t * LANES, (t + 1) * LANES)
                pair = [tile[:points, span], tile[points:, span]]
                largest = jnp.maximum(jnp.abs(pair[0]), jnp.abs(pair[1]))
                largest = jnp.maximum(jnp.max(largest, axis=1, keepdims=True), 1e-30)
                power = jnp.floor(jnp.log2(largest)) + 1.0
                unit = jnp.exp2(15.0 - power)
                powers = jnp.where(lanes == at * 2 + t, power, powers)
                for comp in range(2):
                    value = jnp.clip(jnp.round(pair[comp] * unit), -TOP, TOP).astype(jnp.int16)
                    packed[kind, :, slot * 2 + t, comp * share : (comp + 1) * share] = (
                        value.reshape(groups, share, LANES)
                    )
        count = 2 * per_group + kind
        if kind:
            coded = powers.astype(jnp.int16).reshape(groups, share, LANES)
            for comp in range(2):
                span = slice(comp * share, (comp + 1) * share)
                packed[kind, :, 2 * per_group, span] = coded
        for n, (dx, dz) in enumerate(others):
            there = group_at(dx, dz)
            tile_copies[kind, n] = pltpu.make_async_remote_copy(
                src_ref=packed.at[kind, there, pl.ds(0, count)],
                dst_ref=landed.at[kind, group, pl.ds(0, count)],
                send_sem=tile_send.at[kind, n],
                recv_sem=tile_recv.at[kind, n],
                device_id=(there, row, y),
                device_id_type=MESH,
            )
            tile_copies[kind, n].start()

    for copy in (*row_copies.values(), *col_copies.values(), *mate_copies.values()):
        copy.wait_send()

    lax.fori_loop(0, kpoints, look_up, 0)

    def decode(held, source):
        unit = jnp.exp2(held[1, source, 2 * per_group].astype(jnp.float32) - 15.0)
        for kind in range(2):
            for slot in range(per_group):
                for t in range(2):
                    k = slot * 2 + t
                    at = kind * per_group * 2 + k
                    value = held[kind, source, k].astype(jnp.float32) * unit[:, at : at + 1]
                    decoded[kind, source * per_group + slot, t] = value

    decode(packed, group)
    for n, (dx, dz) in reversed(list(enumerate(others))):
        for kind in range(2):
            tile_copies[kind, n].wait_recv()
        decode(landed, group_at(-dx % xs, dz))

    def add(step, totals):
        for part in range(UNROLL):
            j = step * UNROLL + part
            held = decoded[0, j]
            held_re, held_im = held[:, :share], held[:, share:]
            new = []
            for q in range(2):
                moved = decoded[1, sources[q, j]]
                moved_re, moved_im = moved[:, :share], moved[:, share:]
                new.append(totals[2 * q] + (held_re * moved_re + held_im * moved_im))
                new.append(totals[2 * q + 1] + (held_im * moved_re - held_re * moved_im))
            totals = tuple(new)
        return totals

    zero = jnp.zeros((2, share, LANES), jnp.float32)
    totals = lax.fori_loop(0, kpoints // UNROLL, add, (zero,) * 4)
    for q in range(2):
        for comp in range(2):
            for t in range(2):
                out_ref[comp, q, 0, :, t, :] = totals[2 * q + comp][t]
    for copy in tile_copies.values():
        copy.wait_send()


def shards(sizes, occ, emp, energies, band_order, imag_times, kq_map, slot_kpoint):
    groups, row_count, col_count = sizes
    per_group, chunk, parts, bands = occ.shape
    width = parts * bands
    share = row_count * chunk // groups
    kpoints = groups * per_group
    dma = pltpu.SemaphoreType.DMA
    totals = pl.pallas_call(
        functools.partial(kernel, sizes),
        out_shape=pltpu.VMEM((2, 2, 1, share, 2, col_count * chunk), jnp.float32),
        in_specs=[pl.BlockSpec(memory_space=pl.ANY)] * 7,
        out_specs=pl.BlockSpec(memory_space=pltpu.VMEM),
        scratch_shapes=[
            pltpu.VMEM((2, *occ.shape), jnp.bfloat16),
            pltpu.VMEM((2 * per_group, bands), jnp.float32),
            pltpu.VMEM((2 * per_group, bands), jnp.int32),
            pltpu.VMEM((2, col_count, per_group, chunk, width), jnp.bfloat16),
            pltpu.VMEM((2, row_count, per_group, chunk, width), jnp.bfloat16),
            pltpu.VMEM((2, groups, 2 * per_group + 1, 2 * share, LANES), jnp.int16),
            pltpu.VMEM((2, groups, 2 * per_group + 1, 2 * share, LANES), jnp.int16),
            pltpu.VMEM((2, kpoints, 2, 2 * share, LANES), jnp.float32),
            pltpu.SMEM(imag_times.shape, jnp.float32),
            pltpu.SMEM(kq_map.shape, jnp.int32),
            pltpu.SMEM(slot_kpoint.shape, jnp.int32),
            pltpu.SMEM((kpoints,), jnp.int32),
            pltpu.SMEM((2, kpoints), jnp.int32),
            dma((2, col_count)),
            dma((2, col_count)),
            dma((2, 4)),
            dma((2, 4)),
            dma((2, 4)),
            dma((2, 4)),
            dma((2, groups)),
            dma((2, groups)),
            dma((9,)),
            pltpu.SemaphoreType.REGULAR((len(RELAY),)),
        ],
        compiler_params=pltpu.CompilerParams(collective_id=0, has_side_effects=True),
        name="polarizability",
    )(occ, emp, energies, band_order, imag_times, kq_map, slot_kpoint)
    return totals * (-1.0 / kpoints)


def solution(mesh):
    sizes = (mesh.shape["kgrp"], mesh.shape["row"], mesh.shape["col"])
    in_specs = (
        P("kgrp", ("row", "col"), None, None),
        P("kgrp", ("row", "col"), None, None),
        P(),
        P(),
        P(),
        P(),
        P(),
    )
    out_specs = P(None, None, "col", "kgrp", None, "row")
    return jax.shard_map(
        functools.partial(shards, sizes),
        mesh=mesh,
        in_specs=in_specs,
        out_specs=out_specs,
        check_vma=False,
    )
```
